768 devices in a mesh: row: 48 (over z, y_hi), col: 16 (over y_lo, x, core).
Axes of the slice: x: 4, y: 8 (y_hi: 4, y_lo: 2; y = y_hi * 2 + y_lo), z: 12, core: 2. Of those that a mesh axis runs over, the one named last changes fastest.
Arguments:
- matrix: bfloat16 [27648, 27648], P('col', 'row'), may hold values from -6 to 6, as said below
- mol_sizes: int32 [108], replicated, may hold values from 128 to 384, as said below
- order: int32 [108], replicated, may hold values from 0 to 107, each once
- pattern: int32 [108, 108], replicated, may hold values 0 or 1
Outputs:
- next_iterate: bfloat16 [576, 27648], P('row', 'col')
The draws below stay inside these ranges and needn't reach their ends.
Inputs may be any that keep to these rules, and one draw needn't show every extreme that they name: matrix is symmetric. mol_sizes sum to 27648; they are multiples of 64.
All inputs are finite; a program needn't handle non-finite values.
Results may differ from the reference program's by a relative error of at most 0.004.
Values may be sent and summed in bfloat16 or wider, within the bound.
A program may use at most 32 MiB of HBM per device.

```python
import jax
import jax.numpy as jnp
from jax import lax

SLAB = 576
N = 27648
NMOL = 108


def draw_matrix(key, part):
    key = jax.random.fold_in(key, 11)
    base = jax.random.normal(key, (N, N), jnp.float32)
    sym = (base + base.T) * 0.70710678
    return jnp.clip(sym, -6.0, 6.0).astype(jnp.bfloat16)


def draw_mol_sizes(key, part):
    key = jax.random.fold_in(key, 7)
    unit_key = jax.random.fold_in(key, 1)
    roll_key = jax.random.fold_in(key, 2)
    pairs = NMOL // 2
    units = jax.random.randint(unit_key, (pairs,), 2, 7)
    if pairs >= 1:
        units = units.at[0].set(6)
    first = 64 * units
    second = 512 - first
    both = jnp.stack([first, second], axis=1).reshape(-1)
    rest = jnp.full((NMOL - 2 * pairs,), 256, dtype=jnp.int32)
    sizes = jnp.concatenate([both.astype(jnp.int32), rest]).astype(jnp.int32)
    offset = jax.random.randint(roll_key, (), 0, NMOL)
    return jnp.roll(sizes, offset).astype(jnp.int32)


def set_ends(values, own_key, least, top_value):
    longest = values.shape.index(max(values.shape))
    spots = []
    for shift in (0, 1):
        where = [jax.random.randint(jax.random.fold_in(own_key, axis), (), 0, length) for axis, length in enumerate(values.shape)]
        where[longest] = (where[longest] + shift) % values.shape[longest]
        spots.append(tuple(where))
    return values.at[spots[0]].set(least).at[spots[1]].set(top_value)


def setup_inputs(seed: int = 0) -> dict:
    arg_keys = jax.random.split(jax.random.key(seed), 5)
    matrix = draw_matrix(jax.random.fold_in(arg_keys[4], 71), 0)
    mol_sizes = draw_mol_sizes(jax.random.fold_in(arg_keys[4], 71), 0)
    order = jax.random.permutation(arg_keys[2], NMOL).astype(jnp.int32)
    pattern = set_ends((jax.random.randint(arg_keys[3], (NMOL, NMOL), 0, 4) < 1).astype(jnp.int32), jax.random.fold_in(arg_keys[3], 1), 0, 1)
    return dict(matrix=matrix, mol_sizes=mol_sizes, order=order, pattern=pattern)


def placement_hot(index, mol_sizes, order):
    count = mol_sizes.shape[0]
    slots = jnp.arange(count, dtype=jnp.int32)
    picks = (order[:, None] == slots[None, :]).astype(jnp.int32)
    sizes_in_order = jnp.sum(picks * mol_sizes[None, :], axis=1)
    position = jnp.sum(picks * slots[:, None], axis=0)
    before = (slots[None, :] < position[:, None]).astype(jnp.int32)
    starts = jnp.sum(before * sizes_in_order[None, :], axis=1)
    inside = (index[:, None] >= starts[None, :]) & (index[:, None] < starts[None, :] + mol_sizes[None, :])
    return inside.astype(jnp.float32)


def reference(matrix, mol_sizes, order, pattern):
    index = jnp.arange(N, dtype=jnp.int32)
    onehot = placement_hot(index, mol_sizes, order)
    link = jnp.maximum(jnp.maximum(pattern, pattern.T), jnp.eye(NMOL, dtype=jnp.int32)).astype(jnp.float32)
    mask = jnp.dot(jnp.dot(onehot[:SLAB], link, precision=lax.Precision.HIGHEST), onehot.T, precision=lax.Precision.HIGHEST)
    slab = matrix[:SLAB]
    square = (jnp.dot(slab, matrix, preferred_element_type=jnp.float32) / N * mask).astype(jnp.bfloat16)
    product = jnp.dot(square, matrix, preferred_element_type=jnp.float32)
    return (mask * (1.5 * slab.astype(jnp.float32) - 0.5 * product)).astype(jnp.bfloat16)
```

```python
import jax
import jax.numpy as jnp
from jax import lax
from jax.experimental import pallas as pl
from jax.experimental.pallas import tpu as pltpu
from jax.sharding import PartitionSpec as P

MESH = pl.DeviceIdType.MESH
BF16, F32 = jnp.bfloat16, jnp.float32
NZ, NYH, NYL, NX = 12, 4, 2, 4
NQ, T = 3, 16
SLAB, DEPTH, TOTAL = 576, 1728, 27648
RIGHT, LEFT = 0, 1


def rdma(src, dst, send, recv, device):
    return pltpu.make_async_remote_copy(
        src_ref=src, dst_ref=dst, send_sem=send, recv_sem=recv, device_id=device, device_id_type=MESH
    )


def iota(shape, dim):
    return lax.broadcasted_iota(jnp.int32, shape, dim)


def dot(a, b, dims):
    return lax.dot_general(a, b, (dims, ((), ())), preferred_element_type=F32)


def kernel(
    a_ref, sizes_ref, order_ref, pattern_ref, out_ref,
    turned, slab, part, c1r, half, c2r, xsum, c3r, sq, prod, rsend, rrecv, zsum, ysend, yrecv, mask_sq, mask_out, own,
    load_recv, load_send, yg_send, ag_recv, ag_send, c1_sem, c2_recv, c2_send, c3_sem, c4_recv, c4_send,
    rs_recv, rs_send, yr_recv, yr_send,
):
    row, col = lax.axis_index("row"), lax.axis_index("col")
    z, yh = row // NYH, lax.rem(row, NYH)
    yl, x, k = col // (2 * NX), lax.rem(col // 2, NX), lax.rem(col, 2)

    def at_z(dz):
        return (lax.rem(z + dz + NZ, NZ) * NYH + yh, col)

    def at_y(d):
        return (z * NYH + lax.rem(yh + d, NYH), col)

    def at_x(xx, kk):
        return (row, yl * 2 * NX + xx * 2 + kk)

    core_mate = (row, col + 1 - 2 * k)
    y_mate = (row, (1 - yl) * 2 * NX + x * 2 + k)
    piece = lax.rem(yh + col, NYH)
    to_col, to_piece = row // 3, lax.rem(row, 3)

    @pl.when(col == 0)
    def _():
        turned[...] = a_ref[:, 0:640].T

    barrier = pltpu.get_barrier_semaphore()
    for device in (at_z(1), at_z(-1), at_y(1), at_y(2), at_y(3), core_mate, y_mate):
        pl.semaphore_signal(barrier, 1, device_id=device, device_id_type=MESH)
    for d in range(1, NX):
        for kk in range(2):
            pl.semaphore_signal(barrier, 1, device_id=at_x(lax.rem(x + d, NX), kk), device_id_type=MESH)

    @pl.when((piece < 3) & ((col > 0) | (3 * col + piece != row)))
    def _():
        pl.semaphore_signal(barrier, 1, device_id=(3 * col + piece, 0), device_id_type=MESH)

    loads = jnp.where(col == 0, jnp.where(row < 3, NZ - 1, NZ), 0)
    pl.semaphore_wait(barrier, 13 + loads)

    def load_rows(q, i):
        return turned.at[pl.ds(pl.multiple_of(48 * i + T * q, T), T)]

    def load(q, i):
        return rdma(load_rows(q, i), slab.at[q, i, to_piece], load_send.at[q, i], load_recv.at[q, to_piece], (i * NYH + yh, to_col))

    def load_self(q):
        return pltpu.make_async_copy(load_rows(q, z), slab.at[q, z, to_piece], load_recv.at[q, to_piece])

    @pl.when(col == 0)
    def _():
        for q in range(NQ):
            def step(t, carry):
                i = lax.rem(z + 6 + t, NZ)

                @pl.when((i != z) | (row >= 3))
                def _():
                    load(q, i).start()

                @pl.when((i == z) & (row < 3))
                def _():
                    load_self(q).start()

                return carry

            lax.fori_loop(0, NZ, step, 0)

    n = sizes_ref.shape[1]
    order = order_ref[...]
    sizes = sizes_ref[...]
    eye = (iota((n, n), 0) == iota((n, n), 1))
    sizes_col = jnp.sum(jnp.where(eye, jnp.broadcast_to(sizes, (n, n)), 0), axis=1, keepdims=True)
    picks_t = iota((n, n), 0) == order
    len_row = jnp.sum(jnp.where(picks_t, jnp.broadcast_to(sizes_col, (n, n)), 0), axis=0, keepdims=True)
    len_b = jnp.broadcast_to(len_row, (n, n))
    start = jnp.sum(jnp.where(iota((n, n), 1) < iota((n, n), 0), len_b, 0), axis=1, keepdims=True)
    end = jnp.sum(jnp.where(iota((n, n), 1) <= iota((n, n), 0), len_b, 0), axis=1, keepdims=True)
    start_row = jnp.sum(jnp.where(eye, jnp.broadcast_to(start, (n, n)), 0), axis=0, keepdims=True)
    end_row = jnp.sum(jnp.where(eye, jnp.broadcast_to(end, (n, n)), 0), axis=0, keepdims=True)
    pattern = pattern_ref[...].astype(F32)
    link = jnp.maximum(jnp.maximum(pattern, pattern.T), eye.astype(F32)).astype(BF16)
    picks = picks_t.astype(F32).astype(BF16)
    by_place = dot(dot(picks, link, ((0,), (0,))).astype(BF16), picks, ((1,), (0,))).astype(BF16)

    def cols_hot(first, count):
        index = first + iota((n, count), 1)
        return ((index >= start) & (index < end)).astype(F32).astype(BF16)

    def rows_hot(index):
        return ((index >= start_row) & (index < end_row)).astype(F32).astype(BF16)

    sq_cols = dot(by_place, cols_hot(row * SLAB, SLAB), ((1,), (0,))).astype(BF16)

    def owned_rows(q, count):
        t = iota((3 * T, count), 0)
        return (3 * x + t // T) * 48 + q * T + lax.rem(t, T)

    for q in range(NQ):
        mask_sq[q] = dot(rows_hot(owned_rows(q, n)), sq_cols, ((1,), (0,)))
    out_cols = dot(by_place, cols_hot(col * DEPTH, DEPTH), ((1,), (0,))).astype(BF16)
    mask_out[...] = dot(rows_hot(row * 12 + iota((T, n), 0)), out_cols, ((1,), (0,)))

    def spread(q, d):
        block = slab.at[q, z, piece]
        return rdma(block, block, yg_send.at[q, d - 1], load_recv.at[q, piece], at_y(d))

    def load_wait(q, j):
        block = slab.at[q, z, j]
        rdma(block, block, yg_send.at[q, 0], load_recv.at[q, j], at_y(1)).wait_recv()

    for q in range(NQ):
        @pl.when(piece < 3)
        def _():
            load_wait(q, piece)
            for d in (2, 1, 3):
                spread(q, d).start()

    def pass_on(q, direction, s):
        b = lax.rem(z + NZ - s + 1, NZ) if direction == RIGHT else lax.rem(z + s - 1, NZ)
        block = slab.at[q, b]
        return rdma(block, block, ag_send.at[q, direction, s - 1], ag_recv.at[q, b], at_z(1 if direction == RIGHT else -1))

    def pass_last(q):
        way = (1, -1, 1 - 2 * k)[q]
        block = slab.at[q, lax.rem(z + NZ - 5 * way, NZ)]
        return rdma(block, block, ag_send.at[q, RIGHT, 5], ag_recv.at[q, lax.rem(z + NZ - 5 * way, NZ)], at_z(way))

    def gather_wait(q, b):
        block = slab.at[q, b]
        rdma(block, block, ag_send.at[q, 0, 0], ag_recv.at[q, b], at_z(1)).wait_recv()

    for q in range(NQ):
        for d in range(1, NYH):
            j = lax.rem(piece + d, NYH)

            @pl.when(j < 3)
            def _():
                load_wait(q, j)

        for direction in (RIGHT, LEFT):
            pass_on(q, direction, 1).start()
    for s in range(2, 7):
        for q in range(NQ):
            gather_wait(q, lax.rem(z + NZ - s + 1, NZ))
            if s < 6:
                pass_on(q, RIGHT, s).start()
            gather_wait(q, lax.rem(z + s - 1, NZ))
            if s < 6:
                pass_on(q, LEFT, s).start()
            else:
                pass_last(q).start()

    sel = (iota((T, 48), 1) == 12 * yh + iota((T, 48), 0)).astype(F32).astype(BF16)
    for j in range(3):
        block = jnp.concatenate([slab[q, z, j] for q in range(NQ)], axis=0)
        own[j] = dot(sel, block, ((1,), (0,)))

    def c1(q):
        return rdma(part.at[q, 1 - k], c1r.at[q], c1_sem.at[0, q], c1_sem.at[1, q], core_mate)

    def c2(q, t):
        return rdma(half.at[q, t], c2r.at[q, x], c2_send.at[q, t], c2_recv.at[q, x], at_x(2 * k + t, k))

    def c3(q):
        return rdma(xsum.at[q], c3r.at[q], c3_sem.at[0, q], c3_sem.at[1, q], y_mate)

    def c4(q, i, device):
        block = sq.at[q, x]
        return rdma(block, block, c4_send.at[q, i], c4_recv.at[q, x], device)

    owner = x // 2 == k
    c4_to = [at_x(lax.rem(x + d, NX), kk) for d in (2, 1, 3) for kk in range(2)] + [core_mate]

    def stage_product(q):
        gather_wait(q, lax.rem(z + 6, NZ))
        total = None
        for j in range(3):
            left = slab[q, :, j].reshape(NZ * T, SLAB)
            right = a_ref[:, SLAB * j : SLAB * j + SLAB]
            term = dot(left, right, ((1,), (1,)))
            total = term if total is None else total + term
        part[q] = total.reshape(2, 6 * T, SLAB)
        c1(q).start()

    def stage_core(q):
        c1(q).wait_recv()
        half[q] = (part[q, k] + c1r[q]).reshape(2, 3 * T, SLAB)
        for t in range(2):
            @pl.when(2 * k + t != x)
            def _():
                c2(q, t).start()

    def stage_x(q):
        @pl.when(owner)
        def _():
            total = half[q, lax.rem(x, 2)]
            for d in range(1, NX):
                xs = lax.rem(x + d, NX)
                rdma(half.at[q, 0], c2r.at[q, xs], c2_send.at[q, 0], c2_recv.at[q, xs], core_mate).wait_recv()
                total = total + c2r[q, xs]
            xsum[q] = total
            c3(q).start()

    def stage_y(q):
        @pl.when(owner)
        def _():
            c3(q).wait_recv()
            total = xsum[q] + c3r[q]
            square = (total / TOTAL * mask_sq[q]).astype(BF16).astype(F32)
            unit = owned_rows(q, SLAB) == row * SLAB + iota((3 * T, SLAB), 1)
            sq[q, x] = jnp.where(unit, square - 1.0, square).astype(BF16)
            for i, device in enumerate(c4_to):
                c4(q, i, device).start()

    def send(q, direction, s, way):
        return rdma(rsend.at[q, direction, s - 1], rrecv.at[q, direction, s - 1], rs_send.at[q, direction, s - 1], rs_recv.at[q, direction, s - 1], at_z(way))

    def way_of(q):
        return (1, -1, 1 - 2 * k)[q]

    def stage_second(q):
        for d in range(NX):
            xs = d

            @pl.when((xs != x) | (xs // 2 != k))
            def _():
                rdma(sq.at[q, xs], sq.at[q, xs], c4_send.at[q, 0], c4_recv.at[q, xs], core_mate).wait_recv()

        left = sq[q].reshape(NZ * T, SLAB)
        prod[q] = dot(left, a_ref[...], ((1,), (0,))).reshape(NZ, T, DEPTH)
        rsend[q, RIGHT, 0] = prod[q, lax.rem(z + 6, NZ)].astype(BF16)
        send(q, RIGHT, 1, way_of(q)).start()

    def stage_ring(q, s):
        if s == 2:
            send(q, RIGHT, 1, way_of(q)).wait_recv()
            got = rrecv[q, RIGHT, 0].astype(F32)
            zero = jnp.zeros_like(got)
            from_left = (got, zero, jnp.where(k == 0, got, zero))[q]
            from_right = (zero, got, jnp.where(k == 0, zero, got))[q]
        for direction in (RIGHT, LEFT):
            way = 1 if direction == RIGHT else -1
            if s > 2:
                send(q, direction, s - 1, way).wait_recv()
                got = rrecv[q, direction, s - 2].astype(F32)
            else:
                got = from_left if direction == RIGHT else from_right
            d = lax.rem(z + NZ + way * (7 - s), NZ)
            rsend[q, direction, s - 1] = (prod[q, d] + got).astype(BF16)
            send(q, direction, s, way).start()

    def stage_last(q):
        total = prod[q, z]
        for direction in (RIGHT, LEFT):
            send(q, direction, 6, 1).wait_recv()
            total = total + rrecv[q, direction, 5].astype(F32)
        zsum[T * q : T * q + T] = total

    for stage in (stage_product, stage_core, stage_x, stage_y, stage_second):
        for q in range(NQ):
            stage(q)
    for s in range(2, 7):
        for q in range(NQ):
            stage_ring(q, s)
    for q in range(NQ):
        stage_last(q)

    def y_send(d):
        to = lax.rem(yh + d, NYH)
        return rdma(ysend.at[to], yrecv.at[d - 1], yr_send.at[d - 1], yr_recv.at[d - 1], at_y(d))

    zsum[48:64] = jnp.zeros((T, DEPTH), F32)
    for i in range(NYH):
        ysend[i] = zsum[12 * i : 12 * i + T].astype(BF16)
    for d in (2, 1, 3):
        y_send(d).start()
    total = ysend[yh].astype(F32)
    for d in (1, 3, 2):
        y_send(d).wait_recv()
        total = total + yrecv[d - 1].astype(F32)
    mine = jnp.concatenate([own[j] for j in range(3)], axis=1)
    result = mask_out[...] * (1.5 * mine - 0.5 * (mine + total))
    out_ref[...] = result[:12].astype(BF16)

    @pl.when(col == 0)
    def _():
        for q in range(NQ):
            def step(t, carry):
                @pl.when((t != z) | (row >= 3))
                def _():
                    load(q, t).wait_send()

                return carry

            lax.fori_loop(0, NZ, step, 0)

    for q in range(NQ):
        @pl.when(piece < 3)
        def _():
            for d in range(1, NYH):
                spread(q, d).wait_send()

        for s in range(1, 6):
            for direction in (RIGHT, LEFT):
                pass_on(q, direction, s).wait_send()
        pass_last(q).wait_send()
        c1(q).wait_send()
        for t in range(2):
            @pl.when(2 * k + t != x)
            def _():
                c2(q, t).wait_send()

        @pl.when(owner)
        def _():
            c3(q).wait_send()
            for i, device in enumerate(c4_to):
                c4(q, i, device).wait_send()

        send(q, RIGHT, 1, 1).wait_send()
        for s in range(2, 7):
            for direction in (RIGHT, LEFT):
                send(q, direction, s, 1).wait_send()
    for d in range(1, NYH):
        y_send(d).wait_send()


def local(matrix, mol_sizes, order, pattern):
    vmem = pl.BlockSpec(memory_space=pltpu.VMEM)
    dma = pltpu.SemaphoreType.DMA
    return pl.pallas_call(
        kernel,
        out_shape=jax.ShapeDtypeStruct((12, DEPTH), BF16),
        in_specs=[vmem] * 4,
        out_specs=vmem,
        scratch_shapes=[
            pltpu.VMEM((640, SLAB), BF16),
            pltpu.VMEM((NQ, NZ, 3, T, SLAB), BF16),
            pltpu.VMEM((NQ, 2, 6 * T, SLAB), F32),
            pltpu.VMEM((NQ, 6 * T, SLAB), F32),
            pltpu.VMEM((NQ, 2, 3 * T, SLAB), F32),
            pltpu.VMEM((NQ, NX, 3 * T, SLAB), F32),
            pltpu.VMEM((NQ, 3 * T, SLAB), F32),
            pltpu.VMEM((NQ, 3 * T, SLAB), F32),
            pltpu.VMEM((NQ, NX, 3 * T, SLAB), BF16),
            pltpu.VMEM((NQ, NZ, T, DEPTH), F32),
            pltpu.VMEM((NQ, 2, 6, T, DEPTH), BF16),
            pltpu.VMEM((NQ, 2, 6, T, DEPTH), BF16),
            pltpu.VMEM((64, DEPTH), F32),
            pltpu.VMEM((NYH, T, DEPTH), BF16),
            pltpu.VMEM((NYH - 1, T, DEPTH), BF16),
            pltpu.VMEM((NQ, 3 * T, SLAB), F32),
            pltpu.VMEM((T, DEPTH), F32),
            pltpu.VMEM((3, T, SLAB), F32),
            dma((NQ, 3)),
            dma((NQ, NZ)),
            dma((NQ, 3)),
            dma((NQ, NZ)),
            dma((NQ, 2, 6)),
            dma((2, NQ)),
            dma((NQ, NX)),
            dma((NQ, 2)),
            dma((2, NQ)),
            dma((NQ, NX)),
            dma((NQ, 7)),
            dma((NQ, 2, 6)),
            dma((NQ, 2, 6)),
            dma((3,)),
            dma((3,)),
        ],
        compiler_params=pltpu.CompilerParams(collective_id=0, has_side_effects=True, vmem_limit_bytes=48 << 20),
        name="sign_step",
    )(matrix.T, mol_sizes.reshape(1, -1), order.reshape(1, -1), pattern)


def solution(mesh):
    return jax.shard_map(
        local,
        mesh=mesh,
        in_specs=(P("col", "row"), P(), P(), P()),
        out_specs=P("row", "col"),
        check_vma=False,
    )
```

```python
import functools

import jax
import jax.numpy as jnp
from jax import lax
from jax.experimental import pallas as pl
from jax.experimental.pallas import tpu as pltpu
from jax.sharding import PartitionSpec as P

MESH = pl.DeviceIdType.MESH
BF16, F32 = jnp.bfloat16, jnp.float32
NZ, NYH, NYL, NX = 12, 4, 2, 4
NQ, T = 3, 16
SLAB, DEPTH, TOTAL = 576, 1728, 27648
RIGHT, LEFT = 0, 1
VMEM_MIB = 62
DL = 2.7
GO = (0.0, 1.3, 2.6)
GS = (3.9, 3.9, 3.9)
COL = (0.0, 2.0, 6.0, 10.0, 12.0)
RS = (3.9, 3.9, 3.9)


def rdma(src, dst, send, recv, device):
    return pltpu.make_async_remote_copy(
        src_ref=src, dst_ref=dst, send_sem=send, recv_sem=recv, device_id=device, device_id_type=MESH
    )


def iota(shape, dim):
    return lax.broadcasted_iota(jnp.int32, shape, dim)


def dot(a, b, dims):
    return lax.dot_general(a, b, (dims, ((), ())), preferred_element_type=F32)


def kernel(
    a_hbm, sizes_hbm, order_hbm, pattern_hbm, out_ref,
    a_ref, sizes_ref, order_ref, pattern_ref, turned, dealt, slab, part, c1r, exact, half, c2r, sq, prod, rsend, rrecv, zsum, ysend, yrecv, mask_sq, mask_out, own,
    in_sem, feed_recv, feed_send, load_recv, load_send, yg_send, ag_recv, ag_send, c1_sem, c2_recv, c2_send, c4_recv, c4_send, c5_sem,
    rs_recv, rs_send, yr_recv, yr_send,
):
    row, col = lax.axis_index("row"), lax.axis_index("col")
    z, yh = row // NYH, lax.rem(row, NYH)
    yl, x, k = col // (2 * NX), lax.rem(col // 2, NX), lax.rem(col, 2)

    def at_z(dz):
        return (lax.rem(z + dz + NZ, NZ) * NYH + yh, col)

    def at_y(d):
        return (z * NYH + lax.rem(yh + d, NYH), col)

    def at_x(xx, yy):
        return (row, yy * 2 * NX + xx * 2 + k)

    operands = [
        pltpu.make_async_copy(src, dst, in_sem.at[i])
        for i, (src, dst) in enumerate(
            ((a_hbm, a_ref), (sizes_hbm, sizes_ref), (order_hbm, order_ref), (pattern_hbm, pattern_ref))
        )
    ]
    core_mate = (row, col + 1 - 2 * k)
    piece = lax.rem(yh + col, NYH)
    hub = col == row // 3
    deal = lax.rem(row, 3)


    barrier = pltpu.get_barrier_semaphore()
    for device in (at_z(1), at_z(-1), at_y(1), at_y(2), at_y(3), core_mate):
        pl.semaphore_signal(barrier, 1, device_id=device, device_id_type=MESH)
    for d in range(1, NX):
        pl.semaphore_signal(barrier, 1, device_id=at_x(lax.rem(x + d, NX), yl), device_id_type=MESH)
    for d in range(NX):
        pl.semaphore_signal(barrier, 1, device_id=at_x(lax.rem(x + d, NX), 1 - yl), device_id_type=MESH)

    @pl.when((piece < 3) & (3 * col + piece != row))
    def _():
        pl.semaphore_signal(barrier, 1, device_id=(3 * col + piece, col), device_id_type=MESH)

    @pl.when(hub & (col > 0))
    def _():
        pl.semaphore_signal(barrier, 1, device_id=(row, 0), device_id_type=MESH)

    for copy in operands:
        copy.start()
    operands[0].wait()

    @pl.when(col == 0)
    def _():
        turned[...] = a_ref[:, 0:640].T[:SLAB].reshape(NZ, NQ, T, SLAB)

    extra = jnp.where(hub, NZ - 1, 0) + jnp.where((col == 0) & (row >= 3), 1, 0)
    pl.semaphore_wait(barrier, 13 + extra)

    def feed(q, g):
        part_of = pl.ds(4 * g, 4)
        return rdma(turned.at[part_of, q], dealt.at[q, part_of], feed_send.at[q, g], feed_recv.at[q, g], (row, row // 3))

    def feed_self(q, g):
        part_of = pl.ds(4 * g, 4)
        return pltpu.make_async_copy(turned.at[part_of, q], dealt.at[q, part_of], feed_recv.at[q, g])

    def group(t):
        return lax.rem(z // 4 + 1 + t, 3)

    @pl.when((col == 0) & (row >= 3))
    def _():
        for q in range(NQ):
            for t in range(3):
                feed(q, group(t)).start()

    @pl.when((col == 0) & (row < 3))
    def _():
        for q in range(NQ):
            for t in range(3):
                feed_self(q, group(t)).start()

    def load(q, i):
        return rdma(dealt.at[q, i], slab.at[q, i, deal], load_send.at[q, i], load_recv.at[q, deal], (i * NYH + yh, col))

    def load_self(q):
        return pltpu.make_async_copy(dealt.at[q, z], slab.at[q, z, deal], load_recv.at[q, deal])

    def stage_load(q):
        @pl.when(hub)
        def _():
            for t in range(3):
                g = group(t)
                part_of = dealt.at[q, pl.ds(4 * g, 4)]
                pltpu.make_async_copy(part_of, part_of, feed_recv.at[q, g]).wait()
                for u in range(4):
                    i = 4 * g + u

                    @pl.when(i != z)
                    def _():
                        load(q, i).start()

                    @pl.when(i == z)
                    def _():
                        load_self(q).start()

    for copy in operands[1:]:
        copy.wait()
    n = sizes_ref.shape[1]
    order = order_ref[...]
    sizes = sizes_ref[...]
    eye = (iota((n, n), 0) == iota((n, n), 1))
    sizes_col = jnp.sum(jnp.where(eye, jnp.broadcast_to(sizes, (n, n)), 0), axis=1, keepdims=True)
    picks_t = iota((n, n), 0) == order
    len_row = jnp.sum(jnp.where(picks_t, jnp.broadcast_to(sizes_col, (n, n)), 0), axis=0, keepdims=True)
    len_b = jnp.broadcast_to(len_row, (n, n))
    start = jnp.sum(jnp.where(iota((n, n), 1) < iota((n, n), 0), len_b, 0), axis=1, keepdims=True)
    end = jnp.sum(jnp.where(iota((n, n), 1) <= iota((n, n), 0), len_b, 0), axis=1, keepdims=True)
    start_row = jnp.sum(jnp.where(eye, jnp.broadcast_to(start, (n, n)), 0), axis=0, keepdims=True)
    end_row = jnp.sum(jnp.where(eye, jnp.broadcast_to(end, (n, n)), 0), axis=0, keepdims=True)
    pattern = pattern_ref[...].astype(F32)
    link = jnp.maximum(jnp.maximum(pattern, pattern.T), eye.astype(F32)).astype(BF16)
    picks = picks_t.astype(F32).astype(BF16)
    by_place = dot(dot(picks, link, ((0,), (0,))).astype(BF16), picks, ((1,), (0,))).astype(BF16)

    def cols_hot(first, count):
        index = first + iota((n, count), 1)
        return ((index >= start) & (index < end)).astype(F32).astype(BF16)

    def rows_hot(index):
        return ((index >= start_row) & (index < end_row)).astype(F32).astype(BF16)

    sq_cols = dot(by_place, cols_hot(row * SLAB, SLAB), ((1,), (0,))).astype(BF16)

    def owned_rows(q, xs, count):
        t = iota((3 * T, count), 0)
        return (3 * xs + t // T) * 48 + q * T + lax.rem(t, T)

    def unit(q, xs):
        return owned_rows(q, xs, SLAB) == row * SLAB + iota((3 * T, SLAB), 1)

    for q in range(NQ):
        mask_sq[q] = dot(rows_hot(owned_rows(q, x, n)), sq_cols, ((1,), (0,)))
    out_cols = dot(by_place, cols_hot(col * DEPTH, DEPTH), ((1,), (0,))).astype(BF16)
    mask_out[...] = dot(rows_hot(row * 12 + iota((T, n), 0)), out_cols, ((1,), (0,)))

    def spread(q, d):
        block = slab.at[q, z, piece]
        return rdma(block, block, yg_send.at[q, d - 1], load_recv.at[q, piece], at_y(d))

    def load_wait(q, j):
        block = slab.at[q, z, j]
        rdma(block, block, yg_send.at[q, 0], load_recv.at[q, j], at_y(1)).wait_recv()

    def stage_spread(q):
        @pl.when(piece < 3)
        def _():
            load_wait(q, piece)
            for d in (2, 1, 3):
                spread(q, d).start()

    def pass_on(q, direction, s):
        b = lax.rem(z + NZ - s + 1, NZ) if direction == RIGHT else lax.rem(z + s - 1, NZ)
        block = slab.at[q, b]
        return rdma(block, block, ag_send.at[q, direction, s - 1], ag_recv.at[q, b], at_z(1 if direction == RIGHT else -1))

    def pass_last(q):
        way = (1, -1, 1 - 2 * k)[q]
        block = slab.at[q, lax.rem(z + NZ - 5 * way, NZ)]
        return rdma(block, block, ag_send.at[q, RIGHT, 5], ag_recv.at[q, lax.rem(z + NZ - 5 * way, NZ)], at_z(way))

    def gather_wait(q, b):
        block = slab.at[q, b]
        rdma(block, block, ag_send.at[q, 0, 0], ag_recv.at[q, b], at_z(1)).wait_recv()

    def stage_gather(q, s):
        if s == 1:
            for d in range(1, NYH):
                j = lax.rem(piece + d, NYH)

                @pl.when(j < 3)
                def _():
                    load_wait(q, j)

            for direction in (RIGHT, LEFT):
                pass_on(q, direction, 1).start()
            return
        gather_wait(q, lax.rem(z + NZ - s + 1, NZ))
        if s < 6:
            pass_on(q, RIGHT, s).start()
        gather_wait(q, lax.rem(z + s - 1, NZ))
        if s < 6:
            pass_on(q, LEFT, s).start()
        else:
            pass_last(q).start()

    def stage_own():
        sel = (iota((T, 48), 1) == 12 * yh + iota((T, 48), 0)).astype(F32).astype(BF16)
        rows = []
        for j in range(3):
            block = jnp.concatenate([slab[q, z, j] for q in range(NQ)], axis=0)
            rows.append(dot(sel, block, ((1,), (0,))))
        own[...] = jnp.concatenate(rows, axis=1)

    def c1(q):
        return rdma(part.at[q, 1 - k], c1r.at[q], c1_sem.at[0, q], c1_sem.at[1, q], core_mate)

    def c2(q, t, yy):
        slot = yl * NX + x
        return rdma(half.at[q, t], c2r.at[q, slot], c2_send.at[q, t, lax.rem(yl + yy, 2)], c2_recv.at[q, slot], at_x(2 * k + t, lax.rem(yl + yy, 2)))

    def c4(q, d):
        block = sq.at[q, x]
        return rdma(block, block, c4_send.at[q, d - 1], c4_recv.at[q, x], at_x(lax.rem(x + d, NX), yl))

    def c5(q):
        blocks = sq.at[q, pl.ds(2 * k, 2)]
        return rdma(blocks, blocks, c5_sem.at[0, q], c5_sem.at[1, q], core_mate)

    owner = x // 2 == k

    def stage_product(q):
        gather_wait(q, lax.rem(z + 6, NZ))
        total = None
        for j in range(3):
            left = slab[q, :, j].reshape(NZ * T, SLAB)
            right = a_ref[:, SLAB * j : SLAB * j + SLAB]
            term = dot(left, right, ((1,), (1,)))
            total = term if total is None else total + term
        part[q] = total.reshape(2, 6 * T, SLAB)
        c1(q).start()

    def stage_core(q):
        c1(q).wait_recv()
        total = (part[q, k] + c1r[q]).reshape(2, 3 * T, SLAB)
        for t in range(2):
            block = jnp.where(unit(q, 2 * k + t), total[t] - TOTAL / (NX * NYL), total[t])
            exact[q, t] = block
            half[q, t] = block.astype(BF16)
        for t in range(2):
            c2(q, t, 1).start()

            @pl.when(2 * k + t != x)
            def _():
                c2(q, t, 0).start()

    def stage_sum(q):
        @pl.when(owner)
        def _():
            total = exact[q, lax.rem(x, 2)]
            for d in range(1, NX * NYL):
                slot = lax.rem(yl * NX + x + d, NX * NYL)
                rdma(half.at[q, 0], c2r.at[q, slot], c2_send.at[q, 0, 0], c2_recv.at[q, slot], core_mate).wait_recv()
                total = total + c2r[q, slot].astype(F32)
            one = jnp.where(unit(q, x), 1.0, 0.0)
            square = ((total / TOTAL + one) * mask_sq[q]).astype(BF16).astype(F32)
            sq[q, x] = (square - one).astype(BF16)
            for d in (2, 1, 3):
                c4(q, d).start()

    def send(q, direction, s, way):
        return rdma(rsend.at[q, direction, s - 1], rrecv.at[q, direction, s - 1], rs_send.at[q, direction, s - 1], rs_recv.at[q, direction, s - 1], at_z(way))

    def way_of(q):
        return (1, -1, 1 - 2 * k)[q]

    def stage_mate(q):
        for t in range(2):
            xs = 2 * k + t

            @pl.when(xs != x)
            def _():
                rdma(sq.at[q, xs], sq.at[q, xs], c4_send.at[q, 0], c4_recv.at[q, xs], core_mate).wait_recv()

        c5(q).start()

    def stage_second(q):
        c5(q).wait_recv()
        left = sq[q].reshape(NZ * T, SLAB)
        prod[q] = dot(left, a_ref[...], ((1,), (0,))).reshape(NZ, T, DEPTH)
        rsend[q, RIGHT, 0] = prod[q, lax.rem(z + 6, NZ)].astype(BF16)
        send(q, RIGHT, 1, way_of(q)).start()

    def stage_ring(q, s):
        if s == 2:
            send(q, RIGHT, 1, way_of(q)).wait_recv()
            got = rrecv[q, RIGHT, 0].astype(F32)
            zero = jnp.zeros_like(got)
            from_left = (got, zero, jnp.where(k == 0, got, zero))[q]
            from_right = (zero, got, jnp.where(k == 0, zero, got))[q]
        for direction in (RIGHT, LEFT):
            way = 1 if direction == RIGHT else -1
            if s > 2:
                send(q, direction, s - 1, way).wait_recv()
                got = rrecv[q, direction, s - 2].astype(F32)
            else:
                got = from_left if direction == RIGHT else from_right
            d = lax.rem(z + NZ + way * (7 - s), NZ)
            rsend[q, direction, s - 1] = (prod[q, d] + got).astype(BF16)
            send(q, direction, s, way).start()

    def stage_last(q):
        total = prod[q, z]
        for direction in (RIGHT, LEFT):
            send(q, direction, 6, 1).wait_recv()
            total = total + rrecv[q, direction, 5].astype(F32)
        zsum[T * q : T * q + T] = total

    events = []
    for q in range(NQ):
        at = 10.0 + GO[q]
        plan = [(DL * q, stage_load), (5.0 + DL * q, stage_spread)]
        plan += [(at + GS[q] * (i - 1), functools.partial(stage_gather, s=i)) for i in range(1, 7)]
        at += GS[q] * 6
        plan += zip([at + t for t in COL], [stage_product, stage_core, stage_sum, stage_mate, stage_second])
        at += COL[-1]
        plan += [(at + RS[q] * (i - 1), functools.partial(stage_ring, s=i)) for i in range(2, 7)]
        plan += [(at + RS[q] * 6, stage_last)]
        events += [(when, q, i, stage) for i, (when, stage) in enumerate(plan)]
    for when, q, i, stage in sorted(events, key=lambda e: e[:3]):
        stage(q)
        if (q, i) == (NQ - 1, 2):
            stage_own()

    def y_send(d):
        to = lax.rem(yh + d, NYH)
        return rdma(ysend.at[to], yrecv.at[d - 1], yr_send.at[d - 1], yr_recv.at[d - 1], at_y(d))

    zsum[48:64] = jnp.zeros((T, DEPTH), F32)
    for i in range(NYH):
        ysend[i] = zsum[12 * i : 12 * i + T].astype(BF16)
    for d in (2, 1, 3):
        y_send(d).start()
    total = ysend[yh].astype(F32)
    for d in (1, 3, 2):
        y_send(d).wait_recv()
        total = total + yrecv[d - 1].astype(F32)
    mine = own[...]
    result = mask_out[...] * (1.5 * mine - 0.5 * (mine + total))
    out_ref[...] = result[:12].astype(BF16)

    @pl.when((col == 0) & (row >= 3))
    def _():
        for q in range(NQ):
            for g in range(3):
                feed(q, g).wait_send()

    @pl.when(hub)
    def _():
        for q in range(NQ):
            for i in range(NZ):
                @pl.when(i != z)
                def _():
                    load(q, i).wait_send()

    for q in range(NQ):
        @pl.when(piece < 3)
        def _():
            for d in range(1, NYH):
                spread(q, d).wait_send()

        for s in range(1, 6):
            for direction in (RIGHT, LEFT):
                pass_on(q, direction, s).wait_send()
        pass_last(q).wait_send()
        c1(q).wait_send()
        for t in range(2):
            c2(q, t, 1).wait_send()

            @pl.when(2 * k + t != x)
            def _():
                c2(q, t, 0).wait_send()

        @pl.when(owner)
        def _():
            for d in range(1, NX):
                c4(q, d).wait_send()

        c5(q).wait_send()

        send(q, RIGHT, 1, 1).wait_send()
        for s in range(2, 7):
            for direction in (RIGHT, LEFT):
                send(q, direction, s, 1).wait_send()
    for d in range(1, NYH):
        y_send(d).wait_send()


def local(matrix, mol_sizes, order, pattern):
    count = mol_sizes.shape[0]
    dma = pltpu.SemaphoreType.DMA
    return pl.pallas_call(
        kernel,
        out_shape=jax.ShapeDtypeStruct((12, DEPTH), BF16),
        in_specs=[pl.BlockSpec(memory_space=pl.ANY)] * 4,
        out_specs=pl.BlockSpec(memory_space=pltpu.VMEM),
        scratch_shapes=[
            pltpu.VMEM((SLAB, DEPTH), BF16),
            pltpu.VMEM((1, count), jnp.int32),
            pltpu.VMEM((1, count), jnp.int32),
            pltpu.VMEM((count, count), jnp.int32),
            pltpu.VMEM((NZ, NQ, T, SLAB), BF16),
            pltpu.VMEM((NQ, NZ, T, SLAB), BF16),
            pltpu.VMEM((NQ, NZ, 3, T, SLAB), BF16),
            pltpu.VMEM((NQ, 2, 6 * T, SLAB), F32),
            pltpu.VMEM((NQ, 6 * T, SLAB), F32),
            pltpu.VMEM((NQ, 2, 3 * T, SLAB), F32),
            pltpu.VMEM((NQ, 2, 3 * T, SLAB), BF16),
            pltpu.VMEM((NQ, NX * NYL, 3 * T, SLAB), BF16),
            pltpu.VMEM((NQ, NX, 3 * T, SLAB), BF16),
            pltpu.VMEM((NQ, NZ, T, DEPTH), F32),
            pltpu.VMEM((NQ, 2, 6, T, DEPTH), BF16),
            pltpu.VMEM((NQ, 2, 6, T, DEPTH), BF16),
            pltpu.VMEM((64, DEPTH), F32),
            pltpu.VMEM((NYH, T, DEPTH), BF16),
            pltpu.VMEM((NYH - 1, T, DEPTH), BF16),
            pltpu.VMEM((NQ, 3 * T, SLAB), F32),
            pltpu.VMEM((T, DEPTH), F32),
            pltpu.VMEM((T, DEPTH), F32),
            dma((4,)),
            dma((NQ, 3)),
            dma((NQ, 3)),
            dma((NQ, 3)),
            dma((NQ, NZ)),
            dma((NQ, 3)),
            dma((NQ, NZ)),
            dma((NQ, 2, 6)),
            dma((2, NQ)),
            dma((NQ, NX * NYL)),
            dma((NQ, 2, 2)),
            dma((NQ, NX)),
            dma((NQ, 3)),
            dma((2, NQ)),
            dma((NQ, 2, 6)),
            dma((NQ, 2, 6)),
            dma((3,)),
            dma((3,)),
        ],
        compiler_params=pltpu.CompilerParams(collective_id=0, has_side_effects=True, vmem_limit_bytes=VMEM_MIB << 20),
        name="sign_step",
    )(matrix.T, mol_sizes.reshape(1, -1), order.reshape(1, -1), pattern)


def solution(mesh):
    return jax.shard_map(
        local,
        mesh=mesh,
        in_specs=(P("col", "row"), P(), P(), P()),
        out_specs=P("row", "col"),
        check_vma=False,
    )
```

```python
import functools

import jax
import jax.numpy as jnp
from jax import lax
from jax.experimental import pallas as pl
from jax.experimental.pallas import tpu as pltpu
from jax.sharding import PartitionSpec as P

MESH = pl.DeviceIdType.MESH
BF16, F32 = jnp.bfloat16, jnp.float32
NZ, NYH, NYL, NX = 12, 4, 2, 4
NQ, T = 3, 16
SLAB, DEPTH, TOTAL = 576, 1728, 27648
RIGHT, LEFT = 0, 1
VMEM_MIB = 62
DL = 2.7
SP = 0.1
GB = 6.0
GO = (0.0, 1.3, 2.6)
GS = (3.9, 3.9, 3.9)
COL = (0.0, 1.0, 5.0, 8.5, 10.0)
RS = (3.9, 3.9, 3.9)


def rdma(src, dst, send, recv, device):
    return pltpu.make_async_remote_copy(
        src_ref=src, dst_ref=dst, send_sem=send, recv_sem=recv, device_id=device, device_id_type=MESH
    )


def iota(shape, dim):
    return lax.broadcasted_iota(jnp.int32, shape, dim)


def dot(a, b, dims):
    return lax.dot_general(a, b, (dims, ((), ())), preferred_element_type=F32)


def kernel(
    a_hbm, sizes_hbm, order_hbm, pattern_hbm, out_ref,
    a_ref, sizes_ref, order_ref, pattern_ref, turned_all, turned, dealt, slab, part, c1r, exact, half, c2r, sq, prod, rsend, rrecv, zsum, ysend, yrecv, mask_sq, mask_out, own,
    in_sem, feed_recv, feed_send, load_recv, load_send, yg_send, ag_recv, ag_send, c1_sem, c2_recv, c2_send, c4_recv, c4_send, c5_sem,
    rs_recv, rs_send, yr_recv, yr_send,
):
    row, col = lax.axis_index("row"), lax.axis_index("col")
    z, yh = row // NYH, lax.rem(row, NYH)
    yl, x, k = col // (2 * NX), lax.rem(col // 2, NX), lax.rem(col, 2)

    def at_z(dz):
        return (lax.rem(z + dz + NZ, NZ) * NYH + yh, col)

    def at_y(d):
        return (z * NYH + lax.rem(yh + d, NYH), col)

    def at_x(xx, yy):
        return (row, yy * 2 * NX + xx * 2 + k)

    operands = [
        pltpu.make_async_copy(src, dst, in_sem.at[i])
        for i, (src, dst) in enumerate(
            ((a_hbm, a_ref), (sizes_hbm, sizes_ref), (order_hbm, order_ref), (pattern_hbm, pattern_ref))
        )
    ]
    core_mate = (row, col + 1 - 2 * k)
    piece = lax.rem(yh + col, NYH)
    hub = col == row // 3
    deal = lax.rem(row, 3)


    barrier = pltpu.get_barrier_semaphore()
    @pl.when((piece < 3) & (3 * col + piece != row))
    def _():
        pl.semaphore_signal(barrier, 1, device_id=(3 * col + piece, col), device_id_type=MESH)

    @pl.when(hub & (col > 0))
    def _():
        pl.semaphore_signal(barrier, 1, device_id=(row, 0), device_id_type=MESH)

    for device in (at_y(2), at_y(1), at_y(3), at_z(1), at_z(-1), core_mate):
        pl.semaphore_signal(barrier, 1, device_id=device, device_id_type=MESH)
    for d in range(1, NX):
        pl.semaphore_signal(barrier, 1, device_id=at_x(lax.rem(x + d, NX), yl), device_id_type=MESH)
    for d in range(NX):
        pl.semaphore_signal(barrier, 1, device_id=at_x(lax.rem(x + d, NX), 1 - yl), device_id_type=MESH)

    for copy in operands:
        copy.start()

    @pl.when(col == 0)
    def _():
        operands[0].wait()
        turned[...] = a_ref[:, 0:640].T[:SLAB].reshape(NZ, NQ, T, SLAB)

    extra = jnp.where(hub, NZ - 1, 0) + jnp.where((col == 0) & (row >= 3), 1, 0)
    pl.semaphore_wait(barrier, 13 + extra)

    def feed(q, g):
        part_of = pl.ds(4 * g, 4)
        return rdma(turned.at[part_of, q], dealt.at[q, part_of], feed_send.at[q, g], feed_recv.at[q, g], (row, row // 3))

    def feed_self(q, g):
        part_of = pl.ds(4 * g, 4)
        return pltpu.make_async_copy(turned.at[part_of, q], dealt.at[q, part_of], feed_recv.at[q, g])

    def group(t):
        return lax.rem(z // 4 + 1 + t, 3)

    @pl.when((col == 0) & (row >= 3))
    def _():
        for q in range(NQ):
            for t in range(3):
                feed(q, group(t)).start()

    @pl.when((col == 0) & (row < 3))
    def _():
        for q in range(NQ):
            for t in range(3):
                feed_self(q, group(t)).start()

    def load(q, i):
        return rdma(dealt.at[q, i], slab.at[q, i, deal], load_send.at[q, i], load_recv.at[q, deal], (i * NYH + yh, col))

    def load_self(q):
        return pltpu.make_async_copy(dealt.at[q, z], slab.at[q, z, deal], load_recv.at[q, deal])

    def stage_load(q):
        @pl.when(hub)
        def _():
            for t in range(3):
                g = group(t)
                part_of = dealt.at[q, pl.ds(4 * g, 4)]
                pltpu.make_async_copy(part_of, part_of, feed_recv.at[q, g]).wait()
                for u in range(4):
                    i = 4 * g + u

                    @pl.when(i != z)
                    def _():
                        load(q, i).start()

                    @pl.when(i == z)
                    def _():
                        load_self(q).start()

    def owned_rows(q, xs, count):
        t = iota((3 * T, count), 0)
        return (3 * xs + t // T) * 48 + q * T + lax.rem(t, T)

    def unit(q, xs):
        return owned_rows(q, xs, SLAB) == row * SLAB + iota((3 * T, SLAB), 1)

    def stage_masks():
        @pl.when(col > 0)
        def _():
            operands[0].wait()

        for copy in operands[1:]:
            copy.wait()
        n = sizes_ref.shape[1]
        order = order_ref[...]
        sizes = sizes_ref[...]
        eye = (iota((n, n), 0) == iota((n, n), 1))
        sizes_col = jnp.sum(jnp.where(eye, jnp.broadcast_to(sizes, (n, n)), 0), axis=1, keepdims=True)
        picks_t = iota((n, n), 0) == order
        len_row = jnp.sum(jnp.where(picks_t, jnp.broadcast_to(sizes_col, (n, n)), 0), axis=0, keepdims=True)
        len_b = jnp.broadcast_to(len_row, (n, n))
        start = jnp.sum(jnp.where(iota((n, n), 1) < iota((n, n), 0), len_b, 0), axis=1, keepdims=True)
        end = jnp.sum(jnp.where(iota((n, n), 1) <= iota((n, n), 0), len_b, 0), axis=1, keepdims=True)
        start_row = jnp.sum(jnp.where(eye, jnp.broadcast_to(start, (n, n)), 0), axis=0, keepdims=True)
        end_row = jnp.sum(jnp.where(eye, jnp.broadcast_to(end, (n, n)), 0), axis=0, keepdims=True)
        pattern = pattern_ref[...].astype(F32)
        link = jnp.maximum(jnp.maximum(pattern, pattern.T), eye.astype(F32)).astype(BF16)
        picks = picks_t.astype(F32).astype(BF16)
        by_place = dot(dot(picks, link, ((0,), (0,))).astype(BF16), picks, ((1,), (0,))).astype(BF16)

        def cols_hot(first, count):
            index = first + iota((n, count), 1)
            return ((index >= start) & (index < end)).astype(F32).astype(BF16)

        def rows_hot(index):
            return ((index >= start_row) & (index < end_row)).astype(F32).astype(BF16)

        sq_cols = dot(by_place, cols_hot(row * SLAB, SLAB), ((1,), (0,))).astype(BF16)

        for q in range(NQ):
            mask_sq[q] = dot(rows_hot(owned_rows(q, x, n)), sq_cols, ((1,), (0,)))
        out_cols = dot(by_place, cols_hot(col * DEPTH, DEPTH), ((1,), (0,))).astype(BF16)
        mask_out[...] = dot(rows_hot(row * 12 + iota((T, n), 0)), out_cols, ((1,), (0,)))
        turned_all[...] = a_ref[...].T

    def spread(q, d):
        block = slab.at[q, z, piece]
        return rdma(block, block, yg_send.at[q, d - 1], load_recv.at[q, piece], at_y(d))

    def load_wait(q, j):
        block = slab.at[q, z, j]
        rdma(block, block, yg_send.at[q, 0], load_recv.at[q, j], at_y(1)).wait_recv()

    def stage_spread(q):
        @pl.when(piece < 3)
        def _():
            load_wait(q, piece)
            for d in (2, 1, 3):
                spread(q, d).start()

    def pass_on(q, direction, s):
        b = lax.rem(z + NZ - s + 1, NZ) if direction == RIGHT else lax.rem(z + s - 1, NZ)
        block = slab.at[q, b]
        return rdma(block, block, ag_send.at[q, direction, s - 1], ag_recv.at[q, b], at_z(1 if direction == RIGHT else -1))

    def pass_last(q):
        way = (1, -1, 1 - 2 * k)[q]
        block = slab.at[q, lax.rem(z + NZ - 5 * way, NZ)]
        return rdma(block, block, ag_send.at[q, RIGHT, 5], ag_recv.at[q, lax.rem(z + NZ - 5 * way, NZ)], at_z(way))

    def gather_wait(q, b):
        block = slab.at[q, b]
        rdma(block, block, ag_send.at[q, 0, 0], ag_recv.at[q, b], at_z(1)).wait_recv()

    def stage_gather(q, s):
        if s == 1:
            for d in range(1, NYH):
                j = lax.rem(piece + d, NYH)

                @pl.when(j < 3)
                def _():
                    load_wait(q, j)

            for direction in (RIGHT, LEFT):
                pass_on(q, direction, 1).start()
            return
        gather_wait(q, lax.rem(z + NZ - s + 1, NZ))
        if s < 6:
            pass_on(q, RIGHT, s).start()
        gather_wait(q, lax.rem(z + s - 1, NZ))
        if s < 6:
            pass_on(q, LEFT, s).start()
        else:
            pass_last(q).start()

    def stage_own():
        sel = (iota((T, 48), 1) == 12 * yh + iota((T, 48), 0)).astype(F32).astype(BF16)
        rows = []
        for j in range(3):
            block = jnp.concatenate([slab[q, z, j] for q in range(NQ)], axis=0)
            rows.append(dot(sel, block, ((1,), (0,))))
        own[...] = jnp.concatenate(rows, axis=1)

    def c1(q):
        return rdma(part.at[q, 1 - k], c1r.at[q], c1_sem.at[0, q], c1_sem.at[1, q], core_mate)

    def c2(q, t, yy):
        slot = yl * NX + x
        return rdma(half.at[q, t], c2r.at[q, slot], c2_send.at[q, t, lax.rem(yl + yy, 2)], c2_recv.at[q, slot], at_x(2 * k + t, lax.rem(yl + yy, 2)))

    def c4(q, d):
        block = sq.at[q, x]
        return rdma(block, block, c4_send.at[q, d - 1], c4_recv.at[q, x], at_x(lax.rem(x + d, NX), yl))

    def c5(q):
        blocks = sq.at[q, pl.ds(2 * k, 2)]
        return rdma(blocks, blocks, c5_sem.at[0, q], c5_sem.at[1, q], core_mate)

    owner = x // 2 == k

    def stage_product(q):
        gather_wait(q, lax.rem(z + 6, NZ))
        total = None
        for j in range(3):
            left = slab[q, :, j].reshape(NZ * T, SLAB)
            right = turned_all[SLAB * j : SLAB * j + SLAB]
            term = dot(left, right, ((1,), (0,)))
            total = term if total is None else total + term
        part[q] = total.reshape(2, 6 * T, SLAB)
        c1(q).start()

    def stage_core(q):
        c1(q).wait_recv()
        total = (part[q, k] + c1r[q]).reshape(2, 3 * T, SLAB)
        for t in range(2):
            block = jnp.where(unit(q, 2 * k + t), total[t] - TOTAL / (NX * NYL), total[t])
            exact[q, t] = block
            half[q, t] = block.astype(BF16)
        for t in range(2):
            c2(q, t, 1).start()

            @pl.when(2 * k + t != x)
            def _():
                c2(q, t, 0).start()

    def stage_sum(q):
        @pl.when(owner)
        def _():
            total = exact[q, lax.rem(x, 2)]
            for d in range(1, NX * NYL):
                slot = lax.rem(yl * NX + x + d, NX * NYL)
                rdma(half.at[q, 0], c2r.at[q, slot], c2_send.at[q, 0, 0], c2_recv.at[q, slot], core_mate).wait_recv()
                total = total + c2r[q, slot].astype(F32)
            one = jnp.where(unit(q, x), 1.0, 0.0)
            square = ((total / TOTAL + one) * mask_sq[q]).astype(BF16).astype(F32)
            sq[q, x] = (square - one).astype(BF16)
            for d in (2, 1, 3):
                c4(q, d).start()

    def send(q, direction, s, way):
        return rdma(rsend.at[q, direction, s - 1], rrecv.at[q, direction, s - 1], rs_send.at[q, direction, s - 1], rs_recv.at[q, direction, s - 1], at_z(way))

    def way_of(q):
        return (1, -1, 1 - 2 * k)[q]

    def stage_mate(q):
        for t in range(2):
            xs = 2 * k + t

            @pl.when(xs != x)
            def _():
                rdma(sq.at[q, xs], sq.at[q, xs], c4_send.at[q, 0], c4_recv.at[q, xs], core_mate).wait_recv()

        c5(q).start()

    def stage_second(q):
        c5(q).wait_recv()
        left = sq[q].reshape(NZ * T, SLAB)
        prod[q] = dot(left, a_ref[...], ((1,), (0,))).reshape(NZ, T, DEPTH)
        rsend[q, RIGHT, 0] = prod[q, lax.rem(z + 6, NZ)].astype(BF16)
        send(q, RIGHT, 1, way_of(q)).start()

    def stage_ring(q, s):
        if s == 2:
            send(q, RIGHT, 1, way_of(q)).wait_recv()
            got = rrecv[q, RIGHT, 0].astype(F32)
            zero = jnp.zeros_like(got)
            from_left = (got, zero, jnp.where(k == 0, got, zero))[q]
            from_right = (zero, got, jnp.where(k == 0, zero, got))[q]
        for direction in (RIGHT, LEFT):
            way = 1 if direction == RIGHT else -1
            if s > 2:
                send(q, direction, s - 1, way).wait_recv()
                got = rrecv[q, direction, s - 2].astype(F32)
            else:
                got = from_left if direction == RIGHT else from_right
            d = lax.rem(z + NZ + way * (7 - s), NZ)
            rsend[q, direction, s - 1] = (prod[q, d] + got).astype(BF16)
            send(q, direction, s, way).start()

    def stage_last(q):
        total = prod[q, z]
        for direction in (RIGHT, LEFT):
            send(q, direction, 6, 1).wait_recv()
            total = total + rrecv[q, direction, 5].astype(F32)
        zsum[T * q : T * q + T] = total

    events = []
    for q in range(NQ):
        at = GB + GO[q]
        plan = [(DL * q, stage_load), (SP + DL * q, stage_spread)]
        plan += [(at + GS[q] * (i - 1), functools.partial(stage_gather, s=i)) for i in range(1, 7)]
        at += GS[q] * 6
        plan += zip([at + t for t in COL], [stage_product, stage_core, stage_sum, stage_mate, stage_second])
        at += COL[-1]
        plan += [(at + RS[q] * (i - 1), functools.partial(stage_ring, s=i)) for i in range(2, 7)]
        plan += [(at + RS[q] * 6, stage_last)]
        events += [(when, q, i, stage) for i, (when, stage) in enumerate(plan)]
    for when, q, i, stage in sorted(events, key=lambda e: e[:3]):
        stage(q)
        if (q, i) == (0, 0):
            stage_masks()
        if (q, i) == (NQ - 1, 2):
            stage_own()

    def y_send(d):
        to = lax.rem(yh + d, NYH)
        return rdma(ysend.at[to], yrecv.at[d - 1], yr_send.at[d - 1], yr_recv.at[d - 1], at_y(d))

    zsum[48:64] = jnp.zeros((T, DEPTH), F32)
    for i in range(NYH):
        ysend[i] = zsum[12 * i : 12 * i + T].astype(BF16)
    for d in (2, 1, 3):
        y_send(d).start()
    total = ysend[yh].astype(F32)
    for d in (1, 3, 2):
        y_send(d).wait_recv()
        total = total + yrecv[d - 1].astype(F32)
    mine = own[...]
    result = mask_out[...] * (1.5 * mine - 0.5 * (mine + total))
    out_ref[...] = result[:12].astype(BF16)

    @pl.when((col == 0) & (row >= 3))
    def _():
        for q in range(NQ):
            for g in range(3):
                feed(q, g).wait_send()

    @pl.when(hub)
    def _():
        for q in range(NQ):
            for i in range(NZ):
                @pl.when(i != z)
                def _():
                    load(q, i).wait_send()

    for q in range(NQ):
        @pl.when(piece < 3)
        def _():
            for d in range(1, NYH):
                spread(q, d).wait_send()

        for s in range(1, 6):
            for direction in (RIGHT, LEFT):
                pass_on(q, direction, s).wait_send()
        pass_last(q).wait_send()
        c1(q).wait_send()
        for t in range(2):
            c2(q, t, 1).wait_send()

            @pl.when(2 * k + t != x)
            def _():
                c2(q, t, 0).wait_send()

        @pl.when(owner)
        def _():
            for d in range(1, NX):
                c4(q, d).wait_send()

        c5(q).wait_send()

        send(q, RIGHT, 1, 1).wait_send()
        for s in range(2, 7):
            for direction in (RIGHT, LEFT):
                send(q, direction, s, 1).wait_send()
    for d in range(1, NYH):
        y_send(d).wait_send()


def local(matrix, mol_sizes, order, pattern):
    count = mol_sizes.shape[0]
    dma = pltpu.SemaphoreType.DMA
    return pl.pallas_call(
        kernel,
        out_shape=jax.ShapeDtypeStruct((12, DEPTH), BF16),
        in_specs=[pl.BlockSpec(memory_space=pl.ANY)] * 4,
        out_specs=pl.BlockSpec(memory_space=pltpu.VMEM),
        scratch_shapes=[
            pltpu.VMEM((SLAB, DEPTH), BF16),
            pltpu.VMEM((1, count), jnp.int32),
            pltpu.VMEM((1, count), jnp.int32),
            pltpu.VMEM((count, count), jnp.int32),
            pltpu.VMEM((DEPTH, SLAB), BF16),
            pltpu.VMEM((NZ, NQ, T, SLAB), BF16),
            pltpu.VMEM((NQ, NZ, T, SLAB), BF16),
            pltpu.VMEM((NQ, NZ, 3, T, SLAB), BF16),
            pltpu.VMEM((NQ, 2, 6 * T, SLAB), F32),
            pltpu.VMEM((NQ, 6 * T, SLAB), F32),
            pltpu.VMEM((NQ, 2, 3 * T, SLAB), F32),
            pltpu.VMEM((NQ, 2, 3 * T, SLAB), BF16),
            pltpu.VMEM((NQ, NX * NYL, 3 * T, SLAB), BF16),
            pltpu.VMEM((NQ, NX, 3 * T, SLAB), BF16),
            pltpu.VMEM((NQ, NZ, T, DEPTH), F32),
            pltpu.VMEM((NQ, 2, 6, T, DEPTH), BF16),
            pltpu.VMEM((NQ, 2, 6, T, DEPTH), BF16),
            pltpu.VMEM((64, DEPTH), F32),
            pltpu.VMEM((NYH, T, DEPTH), BF16),
            pltpu.VMEM((NYH - 1, T, DEPTH), BF16),
            pltpu.VMEM((NQ, 3 * T, SLAB), F32),
            pltpu.VMEM((T, DEPTH), F32),
            pltpu.VMEM((T, DEPTH), F32),
            dma((4,)),
            dma((NQ, 3)),
            dma((NQ, 3)),
            dma((NQ, 3)),
            dma((NQ, NZ)),
            dma((NQ, 3)),
            dma((NQ, NZ)),
            dma((NQ, 2, 6)),
            dma((2, NQ)),
            dma((NQ, NX * NYL)),
            dma((NQ, 2, 2)),
            dma((NQ, NX)),
            dma((NQ, 3)),
            dma((2, NQ)),
            dma((NQ, 2, 6)),
            dma((NQ, 2, 6)),
            dma((3,)),
            dma((3,)),
        ],
        compiler_params=pltpu.CompilerParams(collective_id=0, has_side_effects=True, vmem_limit_bytes=VMEM_MIB << 20),
        name="sign_step",
    )(matrix.T, mol_sizes.reshape(1, -1), order.reshape(1, -1), pattern)


def solution(mesh):
    return jax.shard_map(
        local,
        mesh=mesh,
        in_specs=(P("col", "row"), P(), P(), P()),
        out_specs=P("row", "col"),
        check_vma=False,
    )
```

```python
import functools

import jax
import jax.numpy as jnp
from jax import lax
from jax.experimental import pallas as pl
from jax.experimental.pallas import tpu as pltpu
from jax.sharding import PartitionSpec as P

MESH = pl.DeviceIdType.MESH
BF16, F32 = jnp.bfloat16, jnp.float32
NZ, NYH, NYL, NX = 12, 4, 2, 4
NQ, T = 3, 16
SLAB, DEPTH, TOTAL = 576, 1728, 27648
RIGHT, LEFT = 0, 1
VMEM_MIB = 62
DL = 2.7
SP = 0.1
GB = 6.0
GO = (0.0, 1.3, 2.6)
GS = (3.9, 3.9, 3.9)
COL = (0.0, 1.0, 5.0, 8.5, 10.0)
RS = (3.9, 3.9, 3.9)


def rdma(src, dst, send, recv, device):
    return pltpu.make_async_remote_copy(
        src_ref=src, dst_ref=dst, send_sem=send, recv_sem=recv, device_id=device, device_id_type=MESH
    )


def iota(shape, dim):
    return lax.broadcasted_iota(jnp.int32, shape, dim)


def dot(a, b, dims):
    return lax.dot_general(a, b, (dims, ((), ())), preferred_element_type=F32)


def kernel(
    a_hbm, sizes_hbm, order_hbm, pattern_hbm, out_ref,
    a_ref, sizes_ref, order_ref, pattern_ref, turned_all, turned, dealt, slab, part, c1r, exact, half, c2r, sq, prod, rsend, rrecv, zsum, ysend, yrecv, mask_sq, mask_out, own,
    in_sem, feed_recv, feed_send, load_recv, load_send, yg_send, ag_recv, ag_send, c1_sem, c2_recv, c2_send, c4_recv, c4_send, c5_sem,
    rs_recv, rs_send, yr_recv, yr_send,
):
    row, col = lax.axis_index("row"), lax.axis_index("col")
    z, yh = row // NYH, lax.rem(row, NYH)
    yl, x, k = col // (2 * NX), lax.rem(col // 2, NX), lax.rem(col, 2)

    def at_z(dz):
        return (lax.rem(z + dz + NZ, NZ) * NYH + yh, col)

    def at_y(d):
        return (z * NYH + lax.rem(yh + d, NYH), col)

    def at_x(xx, yy):
        return (row, yy * 2 * NX + xx * 2 + k)

    operands = [
        pltpu.make_async_copy(src, dst, in_sem.at[i])
        for i, (src, dst) in enumerate(
            ((a_hbm, a_ref), (sizes_hbm, sizes_ref), (order_hbm, order_ref), (pattern_hbm, pattern_ref))
        )
    ]
    core_mate = (row, col + 1 - 2 * k)
    piece = lax.rem(yh + col, NYH)
    hub = col == row // 3
    deal = lax.rem(row, 3)


    barrier = pltpu.get_barrier_semaphore()
    @pl.when((piece < 3) & (3 * col + piece != row))
    def _():
        pl.semaphore_signal(barrier, 1, device_id=(3 * col + piece, col), device_id_type=MESH)

    @pl.when(hub & (col > 0))
    def _():
        pl.semaphore_signal(barrier, 1, device_id=(row, 0), device_id_type=MESH)

    for device in (at_y(2), at_y(1), at_y(3), at_z(1), at_z(-1), core_mate):
        pl.semaphore_signal(barrier, 1, device_id=device, device_id_type=MESH)
    for d in range(1, NX):
        pl.semaphore_signal(barrier, 1, device_id=at_x(lax.rem(x + d, NX), yl), device_id_type=MESH)
    for d in range(NX):
        pl.semaphore_signal(barrier, 1, device_id=at_x(lax.rem(x + d, NX), 1 - yl), device_id_type=MESH)

    for copy in operands:
        copy.start()

    @pl.when(col == 0)
    def _():
        operands[0].wait()
        turned[...] = a_ref[:, 0:640].T[:SLAB].reshape(NZ, NQ, T, SLAB)

    extra = jnp.where(hub, NZ - 1, 0) + jnp.where((col == 0) & (row >= 3), 1, 0)
    pl.semaphore_wait(barrier, 13 + extra)

    def feed(q, g):
        part_of = pl.ds(4 * g, 4)
        return rdma(turned.at[part_of, q], dealt.at[q, part_of], feed_send.at[q, g], feed_recv.at[q, g], (row, row // 3))

    def feed_self(q, g):
        part_of = pl.ds(4 * g, 4)
        return pltpu.make_async_copy(turned.at[part_of, q], dealt.at[q, part_of], feed_recv.at[q, g])

    def group(t):
        return lax.rem(z // 4 + 1 + t, 3)

    @pl.when((col == 0) & (row >= 3))
    def _():
        for q in range(NQ):
            for t in range(3):
                feed(q, group(t)).start()

    @pl.when((col == 0) & (row < 3))
    def _():
        for q in range(NQ):
            for t in range(3):
                feed_self(q, group(t)).start()

    def load(q, i):
        return rdma(dealt.at[q, i], slab.at[q, i, deal], load_send.at[q, i], load_recv.at[q, deal], (i * NYH + yh, col))

    def load_self(q):
        return pltpu.make_async_copy(dealt.at[q, z], slab.at[q, z, deal], load_recv.at[q, deal])

    def stage_load(q):
        @pl.when(hub)
        def _():
            for t in range(3):
                g = group(t)
                part_of = dealt.at[q, pl.ds(4 * g, 4)]
                pltpu.make_async_copy(part_of, part_of, feed_recv.at[q, g]).wait()
                for u in range(4):
                    i = 4 * g + u

                    @pl.when(i != z)
                    def _():
                        load(q, i).start()

                    @pl.when(i == z)
                    def _():
                        load_self(q).start()

    def owned_rows(q, xs, count):
        t = iota((3 * T, count), 0)
        return (3 * xs + t // T) * 48 + q * T + lax.rem(t, T)

    def unit(q, xs):
        return owned_rows(q, xs, SLAB) == row * SLAB + iota((3 * T, SLAB), 1)

    def stage_masks():
        @pl.when(col > 0)
        def _():
            operands[0].wait()

        for copy in operands[1:]:
            copy.wait()
        n = sizes_ref.shape[1]
        order = order_ref[...]
        sizes = sizes_ref[...]
        eye = (iota((n, n), 0) == iota((n, n), 1))
        sizes_col = jnp.sum(jnp.where(eye, jnp.broadcast_to(sizes, (n, n)), 0), axis=1, keepdims=True)
        picks_t = iota((n, n), 0) == order
        len_row = jnp.sum(jnp.where(picks_t, jnp.broadcast_to(sizes_col, (n, n)), 0), axis=0, keepdims=True)
        len_b = jnp.broadcast_to(len_row, (n, n))
        start = jnp.sum(jnp.where(iota((n, n), 1) < iota((n, n), 0), len_b, 0), axis=1, keepdims=True)
        end = jnp.sum(jnp.where(iota((n, n), 1) <= iota((n, n), 0), len_b, 0), axis=1, keepdims=True)
        start_row = jnp.sum(jnp.where(eye, jnp.broadcast_to(start, (n, n)), 0), axis=0, keepdims=True)
        end_row = jnp.sum(jnp.where(eye, jnp.broadcast_to(end, (n, n)), 0), axis=0, keepdims=True)
        pattern = pattern_ref[...].astype(F32)
        link = jnp.maximum(jnp.maximum(pattern, pattern.T), eye.astype(F32)).astype(BF16)
        picks = picks_t.astype(F32).astype(BF16)
        by_place = dot(dot(picks, link, ((0,), (0,))).astype(BF16), picks, ((1,), (0,))).astype(BF16)

        def cols_hot(first, count):
            index = first + iota((n, count), 1)
            return ((index >= start) & (index < end)).astype(F32).astype(BF16)

        def rows_hot(index):
            return ((index >= start_row) & (index < end_row)).astype(F32).astype(BF16)

        sq_cols = dot(by_place, cols_hot(row * SLAB, SLAB), ((1,), (0,))).astype(BF16)

        for q in range(NQ):
            mask_sq[q] = dot(rows_hot(owned_rows(q, x, n)), sq_cols, ((1,), (0,)))
        out_cols = dot(by_place, cols_hot(col * DEPTH, DEPTH), ((1,), (0,))).astype(BF16)
        mask_out[...] = dot(rows_hot(row * 12 + iota((T, n), 0)), out_cols, ((1,), (0,)))
        turned_all[...] = a_ref[...].T

    def spread(q, d):
        block = slab.at[q, z, piece]
        return rdma(block, block, yg_send.at[q, d - 1], load_recv.at[q, piece], at_y(d))

    def load_wait(q, j):
        block = slab.at[q, z, j]
        rdma(block, block, yg_send.at[q, 0], load_recv.at[q, j], at_y(1)).wait_recv()

    def stage_spread(q):
        @pl.when(piece < 3)
        def _():
            load_wait(q, piece)
            for d in (2, 1, 3):
                spread(q, d).start()

    def pass_on(q, direction, s):
        b = lax.rem(z + NZ - s + 1, NZ) if direction == RIGHT else lax.rem(z + s - 1, NZ)
        block = slab.at[q, b]
        return rdma(block, block, ag_send.at[q, direction, s - 1], ag_recv.at[q, b], at_z(1 if direction == RIGHT else -1))

    def pass_last(q):
        way = (1, -1, 1 - 2 * k)[q]
        block = slab.at[q, lax.rem(z + NZ - 5 * way, NZ)]
        return rdma(block, block, ag_send.at[q, RIGHT, 5], ag_recv.at[q, lax.rem(z + NZ - 5 * way, NZ)], at_z(way))

    def gather_wait(q, b):
        block = slab.at[q, b]
        rdma(block, block, ag_send.at[q, 0, 0], ag_recv.at[q, b], at_z(1)).wait_recv()

    def stage_gather(q, s):
        if s == 1:
            for d in range(1, NYH):
                j = lax.rem(piece + d, NYH)

                @pl.when(j < 3)
                def _():
                    load_wait(q, j)

            for direction in (RIGHT, LEFT):
                pass_on(q, direction, 1).start()
            return
        gather_wait(q, lax.rem(z + NZ - s + 1, NZ))
        if s < 6:
            pass_on(q, RIGHT, s).start()
        gather_wait(q, lax.rem(z + s - 1, NZ))
        if s < 6:
            pass_on(q, LEFT, s).start()
        else:
            pass_last(q).start()

    def stage_own():
        sel = (iota((T, 48), 1) == 12 * yh + iota((T, 48), 0)).astype(F32).astype(BF16)
        rows = []
        for j in range(3):
            block = jnp.concatenate([slab[q, z, j] for q in range(NQ)], axis=0)
            rows.append(dot(sel, block, ((1,), (0,))))
        own[...] = jnp.concatenate(rows, axis=1)

    def c1(q):
        return rdma(part.at[q, 1 - k], c1r.at[q], c1_sem.at[0, q], c1_sem.at[1, q], core_mate)

    def c2(q, t, yy):
        slot = yl * NX + x
        return rdma(half.at[q, t], c2r.at[q, slot], c2_send.at[q, t, lax.rem(yl + yy, 2)], c2_recv.at[q, slot], at_x(2 * k + t, lax.rem(yl + yy, 2)))

    def c4(q, d):
        block = sq.at[q, x]
        return rdma(block, block, c4_send.at[q, d - 1], c4_recv.at[q, x], at_x(lax.rem(x + d, NX), yl))

    def c5(q):
        blocks = sq.at[q, pl.ds(2 * k, 2)]
        return rdma(blocks, blocks, c5_sem.at[0, q], c5_sem.at[1, q], core_mate)

    owner = x // 2 == k

    def stage_product(q):
        gather_wait(q, lax.rem(z + 6, NZ))
        total = None
        for j in range(3):
            left = slab[q, :, j].reshape(NZ * T, SLAB)
            right = turned_all[SLAB * j : SLAB * j + SLAB]
            term = dot(left, right, ((1,), (0,)))
            total = term if total is None else total + term
        part[q] = total.reshape(2, 6 * T, SLAB)
        c1(q).start()

    def stage_core(q):
        c1(q).wait_recv()
        total = (part[q, k] + c1r[q]).reshape(2, 3 * T, SLAB)
        for t in range(2):
            block = jnp.where(unit(q, 2 * k + t), total[t] - TOTAL / (NX * NYL), total[t])
            exact[q, t] = block
            half[q, t] = block.astype(BF16)
        for t in range(2):
            c2(q, t, 1).start()

            @pl.when(2 * k + t != x)
            def _():
                c2(q, t, 0).start()

    def stage_sum(q):
        @pl.when(owner)
        def _():
            total = exact[q, lax.rem(x, 2)]
            for d in range(1, NX * NYL):
                slot = lax.rem(yl * NX + x + d, NX * NYL)
                rdma(half.at[q, 0], c2r.at[q, slot], c2_send.at[q, 0, 0], c2_recv.at[q, slot], core_mate).wait_recv()
                total = total + c2r[q, slot].astype(F32)
            one = jnp.where(unit(q, x), 1.0, 0.0)
            square = ((total / TOTAL + one) * mask_sq[q]).astype(BF16).astype(F32)
            sq[q, x] = (square - one).astype(BF16)
            for d in (2, 1, 3):
                c4(q, d).start()

    def send(q, direction, s, way):
        return rdma(rsend.at[q, direction, s - 1], rrecv.at[q, direction, s - 1], rs_send.at[q, direction, s - 1], rs_recv.at[q, direction, s - 1], at_z(way))

    def way_of(q):
        return (1, -1, 1 - 2 * k)[q]

    def stage_mate(q):
        for t in range(2):
            xs = 2 * k + t

            @pl.when(xs != x)
            def _():
                rdma(sq.at[q, xs], sq.at[q, xs], c4_send.at[q, 0], c4_recv.at[q, xs], core_mate).wait_recv()

        c5(q).start()

    def stage_second(q):
        c5(q).wait_recv()
        left = sq[q].reshape(NZ * T, SLAB)
        prod[q] = dot(left, a_ref[...], ((1,), (0,))).reshape(NZ, T, DEPTH)
        rsend[q, RIGHT, 0] = prod[q, lax.rem(z + 6, NZ)].astype(BF16)
        send(q, RIGHT, 1, way_of(q)).start()

    def stage_ring(q, s):
        if s == 2:
            send(q, RIGHT, 1, way_of(q)).wait_recv()
            got = rrecv[q, RIGHT, 0].astype(F32)
            zero = jnp.zeros_like(got)
            from_left = (got, zero, jnp.where(k == 0, got, zero))[q]
            from_right = (zero, got, jnp.where(k == 0, zero, got))[q]
        for direction in (RIGHT, LEFT):
            way = 1 if direction == RIGHT else -1
            if s > 2:
                send(q, direction, s - 1, way).wait_recv()
                got = rrecv[q, direction, s - 2].astype(F32)
            else:
                got = from_left if direction == RIGHT else from_right
            d = lax.rem(z + NZ + way * (7 - s), NZ)
            rsend[q, direction, s - 1] = (prod[q, d] + got).astype(BF16)
            send(q, direction, s, way).start()

    def y_send(d):
        to = lax.rem(yh + d, NYH)
        return rdma(ysend.at[to], yrecv.at[d - 1], yr_send.at[d - 1], yr_recv.at[d - 1], at_y(d))

    def y_start(i):
        ysend[i] = zsum[12 * i : 12 * i + T].astype(BF16)
        d = lax.rem(i - yh + NYH, NYH)

        @pl.when(d > 0)
        def _():
            y_send(d).start()

    def stage_last(q):
        total = prod[q, z]
        for direction in (RIGHT, LEFT):
            send(q, direction, 6, 1).wait_recv()
            total = total + rrecv[q, direction, 5].astype(F32)
        zsum[T * q : T * q + T] = total
        if q == NQ - 1:
            zsum[48:64] = jnp.zeros((T, DEPTH), F32)
        for i in ((0,), (1,), (2, 3))[q]:
            y_start(i)

    events = []
    for q in range(NQ):
        at = GB + GO[q]
        plan = [(DL * q, stage_load), (SP + DL * q, stage_spread)]
        plan += [(at + GS[q] * (i - 1), functools.partial(stage_gather, s=i)) for i in range(1, 7)]
        at += GS[q] * 6
        plan += zip([at + t for t in COL], [stage_product, stage_core, stage_sum, stage_mate, stage_second])
        at += COL[-1]
        plan += [(at + RS[q] * (i - 1), functools.partial(stage_ring, s=i)) for i in range(2, 7)]
        plan += [(at + RS[q] * 6, stage_last)]
        events += [(when, q, i, stage) for i, (when, stage) in enumerate(plan)]
    for when, q, i, stage in sorted(events, key=lambda e: e[:3]):
        stage(q)
        if (q, i) == (0, 0):
            stage_masks()
        if (q, i) == (NQ - 1, 2):
            stage_own()

    total = ysend[yh].astype(F32)
    for d in (1, 3, 2):
        y_send(d).wait_recv()
        total = total + yrecv[d - 1].astype(F32)
    mine = own[...]
    result = mask_out[...] * (1.5 * mine - 0.5 * (mine + total))
    out_ref[...] = result[:12].astype(BF16)

    @pl.when((col == 0) & (row >= 3))
    def _():
        for q in range(NQ):
            for g in range(3):
                feed(q, g).wait_send()

    @pl.when(hub)
    def _():
        for q in range(NQ):
            for i in range(NZ):
                @pl.when(i != z)
                def _():
                    load(q, i).wait_send()

    for q in range(NQ):
        @pl.when(piece < 3)
        def _():
            for d in range(1, NYH):
                spread(q, d).wait_send()

        for s in range(1, 6):
            for direction in (RIGHT, LEFT):
                pass_on(q, direction, s).wait_send()
        pass_last(q).wait_send()
        c1(q).wait_send()
        for t in range(2):
            c2(q, t, 1).wait_send()

            @pl.when(2 * k + t != x)
            def _():
                c2(q, t, 0).wait_send()

        @pl.when(owner)
        def _():
            for d in range(1, NX):
                c4(q, d).wait_send()

        c5(q).wait_send()

        send(q, RIGHT, 1, 1).wait_send()
        for s in range(2, 7):
            for direction in (RIGHT, LEFT):
                send(q, direction, s, 1).wait_send()
    for d in range(1, NYH):
        y_send(d).wait_send()


def local(matrix, mol_sizes, order, pattern):
    count = mol_sizes.shape[0]
    dma = pltpu.SemaphoreType.DMA
    return pl.pallas_call(
        kernel,
        out_shape=jax.ShapeDtypeStruct((12, DEPTH), BF16),
        in_specs=[pl.BlockSpec(memory_space=pl.ANY)] * 4,
        out_specs=pl.BlockSpec(memory_space=pltpu.VMEM),
        scratch_shapes=[
            pltpu.VMEM((SLAB, DEPTH), BF16),
            pltpu.VMEM((1, count), jnp.int32),
            pltpu.VMEM((1, count), jnp.int32),
            pltpu.VMEM((count, count), jnp.int32),
            pltpu.VMEM((DEPTH, SLAB), BF16),
            pltpu.VMEM((NZ, NQ, T, SLAB), BF16),
            pltpu.VMEM((NQ, NZ, T, SLAB), BF16),
            pltpu.VMEM((NQ, NZ, 3, T, SLAB), BF16),
            pltpu.VMEM((NQ, 2, 6 * T, SLAB), F32),
            pltpu.VMEM((NQ, 6 * T, SLAB), F32),
            pltpu.VMEM((NQ, 2, 3 * T, SLAB), F32),
            pltpu.VMEM((NQ, 2, 3 * T, SLAB), BF16),
            pltpu.VMEM((NQ, NX * NYL, 3 * T, SLAB), BF16),
            pltpu.VMEM((NQ, NX, 3 * T, SLAB), BF16),
            pltpu.VMEM((NQ, NZ, T, DEPTH), F32),
            pltpu.VMEM((NQ, 2, 6, T, DEPTH), BF16),
            pltpu.VMEM((NQ, 2, 6, T, DEPTH), BF16),
            pltpu.VMEM((64, DEPTH), F32),
            pltpu.VMEM((NYH, T, DEPTH), BF16),
            pltpu.VMEM((NYH - 1, T, DEPTH), BF16),
            pltpu.VMEM((NQ, 3 * T, SLAB), F32),
            pltpu.VMEM((T, DEPTH), F32),
            pltpu.VMEM((T, DEPTH), F32),
            dma((4,)),
            dma((NQ, 3)),
            dma((NQ, 3)),
            dma((NQ, 3)),
            dma((NQ, NZ)),
            dma((NQ, 3)),
            dma((NQ, NZ)),
            dma((NQ, 2, 6)),
            dma((2, NQ)),
            dma((NQ, NX * NYL)),
            dma((NQ, 2, 2)),
            dma((NQ, NX)),
            dma((NQ, 3)),
            dma((2, NQ)),
            dma((NQ, 2, 6)),
            dma((NQ, 2, 6)),
            dma((3,)),
            dma((3,)),
        ],
        compiler_params=pltpu.CompilerParams(collective_id=0, has_side_effects=True, vmem_limit_bytes=VMEM_MIB << 20),
        name="sign_step",
    )(matrix.T, mol_sizes.reshape(1, -1), order.reshape(1, -1), pattern)


def solution(mesh):
    return jax.shard_map(
        local,
        mesh=mesh,
        in_specs=(P("col", "row"), P(), P(), P()),
        out_specs=P("row", "col"),
        check_vma=False,
    )
```
